32 devices in a mesh: center: 8 (over z, x), batch: 4 (over y, core).
Axes of the slice: x: 2, y: 2, z: 4, core: 2. Of those that a mesh axis runs over, the one named last changes fastest.
Arguments:
- centers: bfloat16 [4096, 384], P('center'), may hold values from -4 to 4
- weights: bfloat16 [4096, 512], P('center'), may hold values from -1 to 1
- subset_index: int32 [768], P('center'), may hold values from 0 to 4095, as said below
- basis: bfloat16 [768, 256], P('center'), may hold values from -2 to 2
- damping: float32 [256], replicated, may hold values from 0.2 to 0.95
- stored_train_features: bfloat16 [4, 512, 384], P('batch', 'center'), may hold values from -4 to 4
- pool_labels: bfloat16 [4, 512, 512], P('batch', 'center'), may hold values from -4 to 4
- picks: int32 [4, 16], P('batch', 'center'), may hold values from 0 to 63
Outputs:
- new_weights: bfloat16 [4096, 512], P('center')
- residual: bfloat16 [4, 16, 512], P('batch', 'center')
The draws below stay inside these ranges and needn't reach their ends.
Inputs may be any that keep to these rules, and one draw needn't show every extreme that they name: `subset_index`: the entries are distinct centers; center p is held by index p // 512 of center. Of the 96 entries on one device at most 48 are held by any one index, and in every draw some index holds exactly 48 of the entries of every device.
All inputs are finite; a program needn't handle non-finite values.
Results may differ from the reference program's by a relative error of at most 0.013.
Values may be sent and summed in bfloat16 or wider, within the bound.
A program may use at most 64 MiB of HBM per device.

```python
import math
import jax
import jax.numpy as jnp
from jax import lax

D = 384
C = 512
Q = 256
PC = 512
BS_DEV = 2
POOL_DEV = 64
S_DEV = 96
P_SIZE = 4096
S = 768
CAP = 48
GROUPS = 4
BG = 16
POOL_GROUP = 512
N_CENTER = 8


cluster_count = 256


def cluster_table(key):
    table_key = jax.random.fold_in(key, 13)
    values = jnp.clip(jax.random.normal(table_key, (cluster_count, D), jnp.float32), -4.0, 4.0)
    return values * (18.0 / D) ** 0.5


def feature_values(key, own_constant, leading_shape):
    mean_table = cluster_table(key)
    id_key, noise_key = jax.random.split(jax.random.fold_in(key, own_constant), 2)
    cluster_ids = jax.random.randint(id_key, leading_shape, 0, cluster_count, dtype=jnp.int32)
    full_shape = leading_shape + (D,)
    noise_values = jnp.clip(jax.random.normal(noise_key, full_shape, jnp.float32), -4.0, 4.0)
    values = mean_table[cluster_ids] + noise_values * (0.32 / D) ** 0.5
    return jnp.clip(values, -4.0, 4.0).astype(jnp.bfloat16)


def draw_centers(key, part):
    return feature_values(key, 3, (P_SIZE,))


def draw_stored_train_features(key, part):
    return feature_values(key, 5, (GROUPS, POOL_GROUP))


def draw_weights(key, part):
    first_key = jax.random.fold_in(jax.random.fold_in(key, 17), 0)
    magnitude = float(P_SIZE // 16) ** (-0.5)
    values = jnp.clip(jax.random.normal(first_key, (P_SIZE, C), jnp.float32), -4.0, 4.0)
    values = values * magnitude
    return (values - jnp.roll(values, 1, axis=0)).astype(jnp.bfloat16)


def draw_basis(key, part):
    holders = S // S_DEV
    first_key, second_key = jax.random.split(jax.random.fold_in(key, 7))
    magnitude = 1.2 * float(S * Q) ** (-0.25)
    values = jnp.clip(jax.random.normal(first_key, (S, Q), jnp.float32), -4.0, 4.0)
    pairing = jax.random.permutation(second_key, holders)
    row_holder = jnp.arange(S, dtype=jnp.int32) // S_DEV
    column_block = jnp.arange(Q, dtype=jnp.int32) // (Q // holders)
    spike = jnp.where(pairing[row_holder][:, None] == column_block[None, :], 4.0, 1.0)
    return (values * magnitude * spike).astype(jnp.bfloat16)


def draw_subset_index(key, part):
    holders = S // S_DEV
    slot_count = holders * CAP
    keys = jax.random.split(jax.random.fold_in(key, 11), 4)
    busiest = jax.random.randint(keys[0], (), 0, holders, dtype=jnp.int32)
    owner_bias = jax.random.randint(keys[1], (holders,), 0, 2048, dtype=jnp.int32)
    shuffles = jax.vmap(lambda subkey: jax.random.permutation(subkey, PC))(jax.random.split(keys[2], holders))
    slot_ids = jnp.arange(slot_count, dtype=jnp.int32)
    slot_holder = slot_ids // CAP

    def single_provider(subkey, source):
        jitter_key, order_key = jax.random.split(subkey)
        jitter = jax.random.randint(jitter_key, (slot_count,), 0, 4096, dtype=jnp.int32)
        ranking = owner_bias[slot_holder] + jitter
        ranking = jnp.where(slot_holder == busiest, 16384, ranking)
        ranking = ranking * slot_count + slot_ids
        _, chosen = lax.top_k(ranking, S_DEV)
        chosen = chosen.astype(jnp.int32)
        holder = chosen // CAP
        inside_slice = chosen - holder * CAP
        local_row = shuffles[holder, source * CAP + inside_slice].astype(jnp.int32)
        entries = holder * PC + local_row
        position_order = jax.random.permutation(order_key, S_DEV)
        return entries[position_order]
    sources = jnp.arange(holders, dtype=jnp.int32)
    result = jax.vmap(single_provider)(jax.random.split(keys[3], holders), sources)
    return result.reshape(S).astype(jnp.int32)


def with_ends(values, key, least, largest):
    index_at = [jax.random.randint(jax.random.fold_in(key, axis), (), 0, length) for axis, length in enumerate(values.shape)]
    main_axis = values.shape.index(max(values.shape))
    next_to = index_at[:main_axis] + [(index_at[main_axis] + 1) % values.shape[main_axis]] + index_at[main_axis + 1:]
    return values.at[tuple(index_at)].set(least).at[tuple(next_to)].set(largest)


def steps_of(own_key, shape, pieces, least, largest):
    def one(axis_at, shards_of):
        steps = jax.random.uniform(jax.random.fold_in(jax.random.fold_in(own_key, 6), axis_at), (shards_of,), jnp.float32, least / len(pieces), largest / len(pieces))
        return jnp.repeat(jnp.exp(steps), shape[axis_at] // shards_of).reshape((-1,) + (1,) * (len(shape) - axis_at - 1))

    level = one(*pieces[0])
    for cut in pieces[1:]:
        level = level * one(*cut)
    return level


def bell_draw(rng, dims, deviation, limit, cuts=(), kind=jnp.bfloat16):
    values = deviation * jax.random.normal(rng, dims, jnp.float32)
    if cuts:
        values = values * steps_of(rng, dims, cuts, -0.22, 0.18)
    return jnp.clip(values, -limit, limit).astype(kind)


def setup_inputs(seed: int = 0) -> dict:
    streams_of = jax.random.split(jax.random.key(seed), 9)
    centers = draw_centers(jax.random.fold_in(streams_of[8], 71), 0)
    weights = draw_weights(jax.random.fold_in(streams_of[8], 71), 0)
    subset_index = draw_subset_index(jax.random.fold_in(streams_of[8], 71), 0)
    basis = draw_basis(jax.random.fold_in(streams_of[8], 71), 0)
    damping = jnp.clip(jnp.exp(jax.random.uniform(streams_of[4], (Q,), jnp.float32, math.log(0.2), math.log(0.95))), 0.2, 0.95)
    stored_train_features = draw_stored_train_features(jax.random.fold_in(streams_of[8], 71), 0)
    pool_labels = bell_draw(streams_of[6], (GROUPS, POOL_GROUP, C), 1.0, 4.0, ((0, 4), (1, 8)))
    picks = with_ends(jax.random.randint(streams_of[7], (GROUPS, BG), 0, POOL_DEV), jax.random.fold_in(streams_of[7], 1), 0, POOL_DEV - 1).astype(jnp.int32)
    return dict(centers=centers, weights=weights, subset_index=subset_index, basis=basis, damping=damping, stored_train_features=stored_train_features, pool_labels=pool_labels, picks=picks)


kernel_length = 2.0
step_rate = 0.1

def kernel_block(features, sample_squared_norm, center_rows):
    centers_sq = lax.optimization_barrier(jnp.sum(jnp.square(center_rows.astype(jnp.float32)), axis=1))
    cross = jnp.dot(features, center_rows.T, preferred_element_type=jnp.float32)
    distance = sample_squared_norm[:, None] + centers_sq[None, :] - 2.0 * cross
    return jnp.exp(-jnp.sqrt(jnp.maximum(distance, 0.0)) / kernel_length).astype(jnp.bfloat16)

def reference(centers, weights, subset_index, basis, damping, stored_train_features, pool_labels, picks):
    groups = stored_train_features.shape[0]
    position = jnp.arange(BG, dtype=jnp.int32) // BS_DEV * POOL_DEV
    position = position[None, :] + picks.astype(jnp.int32)
    features = jax.vmap(lambda pool_rows, indices: jnp.take(pool_rows, indices, axis=0))(stored_train_features, position)
    targets = jax.vmap(lambda pool_rows, indices: jnp.take(pool_rows, indices, axis=0))(pool_labels, position)
    flat_features = features.reshape(groups * BG, D)
    sample_squared_norm = lax.optimization_barrier(jnp.sum(jnp.square(flat_features.astype(jnp.float32)), axis=1))
    center_blocks = centers.reshape(N_CENTER, PC, D)
    weight_blocks = weights.reshape(N_CENTER, PC, C)

    def predict(running, operands):
        center_rows, weight_rows = operands
        laplace_kernel = kernel_block(flat_features, sample_squared_norm, center_rows)
        return (running + jnp.dot(laplace_kernel, weight_rows, preferred_element_type=jnp.float32), None)
    predicted, _ = lax.scan(predict, jnp.zeros((groups * BG, C), jnp.float32), (center_blocks, weight_blocks))
    residual = (predicted - targets.reshape(groups * BG, C).astype(jnp.float32)).astype(jnp.bfloat16)
    residual = residual.reshape(groups, BG, C)

    def gradient(running, center_rows):
        laplace_kernel = kernel_block(flat_features, sample_squared_norm, center_rows).reshape(groups, BG, PC)
        subtotal_sums = jnp.einsum('jwy,jwu->jyu', laplace_kernel.astype(jnp.float32), residual.astype(jnp.float32))
        rounded = lax.optimization_barrier(subtotal_sums.astype(jnp.bfloat16))
        return (running, step_rate * lax.optimization_barrier(jnp.sum(rounded.astype(jnp.float32), axis=0)))
    _, grads = lax.scan(gradient, jnp.zeros((), jnp.float32), center_blocks)
    grad = grads.reshape(N_CENTER * PC, C)
    picked = jnp.take(grad, subset_index.astype(jnp.int32), axis=0).astype(jnp.bfloat16)
    projected = lax.dot_general(basis, picked, (((0,), (0,)), ((), ())), preferred_element_type=jnp.float32)
    scaled = (damping[:, None] * projected).astype(jnp.bfloat16)
    correction = jnp.dot(basis, scaled, preferred_element_type=jnp.float32)
    updated = (weights.astype(jnp.float32) - grad).at[subset_index.astype(jnp.int32)].add(correction)
    return (updated.astype(jnp.bfloat16), residual)
```

```python
import functools

import jax
import jax.numpy as jnp
from jax import lax
from jax.experimental import pallas as pl
from jax.experimental.pallas import tpu as pltpu
from jax.sharding import PartitionSpec as P

MESH = pl.DeviceIdType.MESH
kernel_length = 2.0
step_rate = 0.1
LANES = 128
F32, BF16 = jnp.float32, jnp.bfloat16


def dot(a, b, ca=1, cb=0):
    return lax.dot_general(a, b, (((ca,), (cb,)), ((), ())), preferred_element_type=F32)


def each(count, body):
    if count <= 8:
        for k in range(count):
            body(k)
    else:
        lax.fori_loop(0, count, lambda k, c: (body(k), c)[1], 0)


def round_up(x, m):
    return (x + m - 1) // m * m


def laplace(features, sq_centers, center_rows):
    wide = features.astype(F32)
    sq_samples = jnp.sum(wide * wide, axis=1, keepdims=True)
    distance = sq_samples + sq_centers - 2.0 * dot(features, center_rows, 1, 1)
    return jnp.exp(-jnp.sqrt(jnp.maximum(distance, 0.0)) / kernel_length)


def step_kernel(
    n, nb, rank_rows, slot_rows,
    centers_h, weights_h, idx_ref, basis_h, damping_ref, pool_h, labels_h, picks_ref,
    out_w, out_r,
    centers, weights, basis, pool, labels, idx_row,
    feat, feat_f32, feat_all, pack_out, pack_in, place_out, place_in,
    sums_out, sums_in, back, back_f32, back_all,
    local_sem, send_sem, recv_sem,
):
    me, mb = lax.axis_index("center"), lax.axis_index("batch")
    own, D = feat.shape[1:]
    PC, C = weights.shape
    S, Q = basis_h.shape
    SP = basis.shape[0]
    pool_rows = pool.shape[0]
    group = own * n

    loads = [
        pltpu.make_async_copy(src, dst, local_sem.at[i])
        for i, (src, dst) in enumerate(
            [
                (pool_h, pool),
                (basis_h, basis.at[pl.ds(0, S)]),
                (centers_h, centers),
                (labels_h, labels),
                (weights_h, weights),
            ]
        )
    ]
    for load in loads:
        load.start()
    pool_load, basis_load, centers_load, labels_load, weights_load = loads

    def center_peer(k):
        return lax.rem(me + 1 + k, n)

    def batch_peer(k):
        return lax.rem(mb + 1 + k, nb)

    barrier = pltpu.get_barrier_semaphore()

    def greet_center(k):
        pl.semaphore_signal(barrier, inc=1, device_id={"center": center_peer(k)}, device_id_type=MESH)

    def greet_batch(k):
        pl.semaphore_signal(barrier, inc=1, device_id={"batch": batch_peer(k)}, device_id_type=MESH)

    each(n - 1, greet_center)
    each(nb - 1, greet_batch)

    idx_row[...] = jnp.full(idx_row.shape, -1, jnp.int32)
    idx_row[:, 0:S] = idx_ref[...]
    if SP > S:
        basis[pl.ds(S, SP - S), :] = jnp.zeros((SP - S, Q), BF16)
    if slot_rows > rank_rows:
        pack_in[:, pl.ds(rank_rows, slot_rows - rank_rows), :] = jnp.zeros(
            (n, slot_rows - rank_rows, Q), BF16
        )
    idx = idx_row[...]
    nh = round_up(n, 16)
    first = lax.broadcasted_iota(jnp.int32, (nh, SP), 0) * PC
    inside = (idx >= first) & (idx < first + PC) & (first < n * PC)
    member = jnp.where(inside, 1.0, 0.0)
    before = jnp.where(
        lax.broadcasted_iota(jnp.int32, (SP, SP), 0) < lax.broadcasted_iota(jnp.int32, (SP, SP), 1), 1.0, 0.0
    )
    ranks = dot(member.astype(BF16), before.astype(BF16))
    rank = jnp.sum(member * ranks, axis=0, keepdims=True)
    holder = jnp.sum(
        member * lax.broadcasted_iota(jnp.int32, (nh, SP), 0).astype(F32), axis=0, keepdims=True
    )
    real = idx >= 0
    local = idx.astype(F32) - holder * PC
    packed_row = jnp.where(real, holder * rank_rows + rank, -1.0)
    share = LANES // slot_rows
    lane_start = (lax.rem(me, share) * slot_rows).astype(F32)
    code = jnp.where(real, holder * LANES + rank + lane_start, -1.0)
    code_t = jnp.transpose(jnp.broadcast_to(code, (LANES, SP)))
    local_t = jnp.transpose(jnp.broadcast_to(local, (LANES, SP))) + 1.0
    lane = lax.broadcasted_iota(jnp.int32, (SP, LANES), 1).astype(F32)

    def fill_place(h):
        hit = code_t == lane + lax.convert_element_type(h, F32) * LANES
        place_out[h] = jnp.sum(jnp.where(hit, local_t, 0.0), axis=0, keepdims=True)

    each(n, fill_place)
    chosen = lax.broadcasted_iota(jnp.int32, (n * rank_rows, SP), 0).astype(F32) == packed_row
    chosen = jnp.where(chosen, 1.0, 0.0).astype(BF16)

    pool_load.wait()
    lanes = lax.broadcasted_iota(jnp.int32, (8, pool_rows), 1)
    rows = lax.broadcasted_iota(jnp.int32, (8, pool_rows), 0)
    pick = jnp.zeros((8, pool_rows), jnp.bool_)
    for i in range(own):
        pick = pick | ((rows == i) & (lanes == picks_ref[0, i]))
    pick = jnp.where(pick, 1.0, 0.0).astype(BF16)
    feat[me] = dot(pick, pool[...])[0:own]

    basis_load.wait()
    pack_out[...] = dot(chosen, basis[...]).astype(BF16).reshape(n, rank_rows, Q)
    pack_in[me, pl.ds(0, rank_rows), :] = pack_out[me]
    place_in[me] = place_out[me]

    pl.semaphore_wait(barrier, n + nb - 2)

    def send(src, dst, i, device):
        pltpu.make_async_remote_copy(
            src_ref=src,
            dst_ref=dst,
            send_sem=send_sem.at[i],
            recv_sem=recv_sem.at[i],
            device_id=device,
            device_id_type=MESH,
        ).start()

    def finish(sem, i, ref):
        pltpu.make_async_copy(ref, ref, sem.at[i]).wait()

    rest = pl.ds(0, n - 1)
    rest_b = pl.ds(0, nb - 1)
    head = pl.ds(0, rank_rows)

    def send_feat(k):
        send(feat.at[me], feat.at[me], 0, {"center": center_peer(k)})

    def send_pack(k):
        j = center_peer(k)
        send(pack_out.at[j], pack_in.at[me, head], 1, {"center": j})
        send(place_out.at[j], place_in.at[me], 2, {"center": j})

    each(n - 1, send_feat)
    each(n - 1, send_pack)

    labels_load.wait()
    targets = dot(pick, labels[...])[0:own]
    centers_load.wait()
    center_rows = centers[...]
    wide = center_rows.astype(F32)
    square = wide * wide
    high = square.astype(BF16)
    low = (square - high.astype(F32)).astype(BF16)
    ones = jnp.ones((16, D), BF16)
    sq_centers = (dot(ones, high, 1, 1) + dot(ones, low, 1, 1))[0:1]

    finish(recv_sem, 0, feat.at[rest])
    for j in range(n):
        feat_f32[own * j : own * (j + 1), :] = feat[j]
    group_features = feat_f32[...].astype(BF16)
    feat_all[mb] = group_features
    kernel = laplace(group_features, sq_centers, center_rows).astype(BF16)
    weights_load.wait()
    predicted = dot(kernel, weights[...])

    finish(recv_sem, 1, pack_in.at[rest, head])
    finish(recv_sem, 2, place_in.at[rest])
    tiles = []
    for t in range(round_up(n, share) // share):
        row = place_in[t * share]
        for j in range(t * share + 1, min(n, (t + 1) * share)):
            row = row + place_in[j]
        centers_iota = (lax.broadcasted_iota(jnp.int32, (PC, LANES), 0) + 1).astype(F32)
        tiles.append(jnp.where(centers_iota == row, 1.0, 0.0).astype(BF16)[:, : min(n - t * share, share) * slot_rows])
    spread = jnp.concatenate(tiles, axis=1) if len(tiles) > 1 else tiles[0]
    own_basis = dot(spread, pack_in[...].reshape(n * slot_rows, Q)).astype(BF16)
    overlap = dot(kernel, own_basis)

    for j in range(n):
        sums_out[j, :, 0:C] = predicted[own * j : own * (j + 1)]
        sums_out[j, :, C : C + Q] = overlap[own * j : own * (j + 1)]
    sums_in[me] = sums_out[me]

    def send_sums(k):
        j = center_peer(k)
        send(sums_out.at[j], sums_in.at[me], 3, {"center": j})

    def send_group(k):
        send(feat_all.at[mb], feat_all.at[mb], 4, {"batch": batch_peer(k)})

    each(n - 1, send_sums)
    each(nb - 1, send_group)

    finish(recv_sem, 3, sums_in.at[rest])
    total = jnp.sum(sums_in[...], axis=0)
    residual = (total[:, 0:C] - targets).astype(BF16)
    out_r[...] = residual
    back[me, :, 0:C] = residual.astype(F32)
    back[me, :, C : C + Q] = total[:, C:] * damping_ref[...] * step_rate

    def send_back(k):
        send(back.at[me], back.at[me], 5, {"center": center_peer(k)})

    each(n - 1, send_back)

    finish(recv_sem, 4, feat_all.at[rest_b])
    all_features = feat_all[...].reshape(nb * group, D)
    kernel_t = jnp.transpose(laplace(all_features, sq_centers, center_rows)).astype(BF16)

    finish(recv_sem, 5, back.at[rest])
    for j in range(n):
        back_f32[own * j : own * (j + 1), :] = back[j]
    overlap_f32 = back_f32[:, C : C + Q]
    overlap_high = overlap_f32.astype(BF16)
    back_all[mb, :, 0:C] = back_f32[:, 0:C].astype(BF16)
    back_all[mb, :, C : C + Q] = overlap_high
    back_all[mb, :, C + Q : C + 2 * Q] = (overlap_f32 - overlap_high.astype(F32)).astype(BF16)

    def send_back_batch(k):
        send(back_all.at[mb], back_all.at[mb], 6, {"batch": batch_peer(k)})

    each(nb - 1, send_back_batch)
    finish(recv_sem, 6, back_all.at[rest_b])

    everything = back_all[...].reshape(nb * group, C + 2 * Q)
    residuals = everything[:, 0:C]
    scaled = dot(everything[:, C : C + Q], residuals, 0, 0) + dot(everything[:, C + Q :], residuals, 0, 0)
    correction = dot(own_basis, scaled.astype(BF16))
    gradient = step_rate * dot(kernel_t, residuals)
    out_w[...] = ((weights[...].astype(F32) - gradient) + correction).astype(BF16)

    finish(send_sem, 0, feat.at[rest])
    finish(send_sem, 1, pack_in.at[rest, head])
    finish(send_sem, 2, place_in.at[rest])
    finish(send_sem, 3, sums_in.at[rest])
    finish(send_sem, 4, feat_all.at[rest_b])
    finish(send_sem, 5, back.at[rest])
    finish(send_sem, 6, back_all.at[rest_b])


def solution(mesh):
    n, nb = mesh.shape["center"], mesh.shape["batch"]

    def per_device(centers, weights, subset_index, basis, damping, stored, labels, picks):
        (PC, D), C = centers.shape, weights.shape[1]
        S, Q = basis.shape
        SP = round_up(S, LANES)
        own, pool_rows = picks.shape[1], stored.shape[1]
        group = own * n
        capacity = max(1, 4 * S // n)
        rank_rows = round_up(capacity, 16)
        slot_rows = 16
        while slot_rows < rank_rows:
            slot_rows *= 2
        anywhere = pl.BlockSpec(memory_space=pl.ANY)
        vmem = pl.BlockSpec(memory_space=pltpu.VMEM)
        smem = pl.BlockSpec(memory_space=pltpu.SMEM)
        new_weights, residual = pl.pallas_call(
            functools.partial(step_kernel, n, nb, rank_rows, slot_rows),
            out_shape=(
                jax.ShapeDtypeStruct((PC, C), BF16),
                jax.ShapeDtypeStruct((own, C), BF16),
            ),
            in_specs=[anywhere, anywhere, vmem, anywhere, vmem, anywhere, anywhere, smem],
            out_specs=(vmem, vmem),
            scratch_shapes=[
                pltpu.VMEM((PC, D), BF16),
                pltpu.VMEM((PC, C), BF16),
                pltpu.VMEM((SP, Q), BF16),
                pltpu.VMEM((pool_rows, D), BF16),
                pltpu.VMEM((pool_rows, C), BF16),
                pltpu.VMEM((1, SP), jnp.int32),
                pltpu.VMEM((n, own, D), F32),
                pltpu.VMEM((group, D), F32),
                pltpu.VMEM((nb, group, D), BF16),
                pltpu.VMEM((n, rank_rows, Q), BF16),
                pltpu.VMEM((n, slot_rows, Q), BF16),
                pltpu.VMEM((n, 1, LANES), F32),
                pltpu.VMEM((n, 1, LANES), F32),
                pltpu.VMEM((n, own, C + Q), F32),
                pltpu.VMEM((n, own, C + Q), F32),
                pltpu.VMEM((n, own, C + Q), F32),
                pltpu.VMEM((group, C + Q), F32),
                pltpu.VMEM((nb, group, C + 2 * Q), BF16),
                pltpu.SemaphoreType.DMA((5,)),
                pltpu.SemaphoreType.DMA((7,)),
                pltpu.SemaphoreType.DMA((7,)),
            ],
            compiler_params=pltpu.CompilerParams(
                collective_id=0, has_side_effects=True, vmem_limit_bytes=40 * 1024 * 1024
            ),
        )(
            centers,
            weights,
            subset_index.reshape(1, S),
            basis,
            damping.reshape(1, Q),
            stored[0],
            labels[0],
            picks,
        )
        return new_weights, residual[None]

    return jax.shard_map(
        per_device,
        mesh=mesh,
        in_specs=(
            P("center", None),
            P("center", None),
            P("center"),
            P("center", None),
            P(),
            P("batch", "center", None),
            P("batch", "center", None),
            P("batch", "center"),
        ),
        out_specs=(P("center", None), P("batch", "center", None)),
        check_vma=False,
    )
```

```python
import functools

import jax
import jax.numpy as jnp
from jax import lax
from jax.experimental import pallas as pl
from jax.experimental.pallas import tpu as pltpu
from jax.sharding import PartitionSpec as P

MESH = pl.DeviceIdType.MESH
kernel_length = 2.0
step_rate = 0.1
LANES = 128
F32, BF16 = jnp.float32, jnp.bfloat16


def dot(a, b, ca=1, cb=0):
    return lax.dot_general(a, b, (((ca,), (cb,)), ((), ())), preferred_element_type=F32)


def each(count, body):
    if count <= 8:
        for k in range(count):
            body(k)
    else:
        lax.fori_loop(0, count, lambda k, c: (body(k), c)[1], 0)


def round_up(x, m):
    return (x + m - 1) // m * m


def laplace(features, sq_centers, centers_t):
    wide = features.astype(F32)
    sq_samples = jnp.sum(wide * wide, axis=1, keepdims=True)
    distance = sq_samples + sq_centers - 2.0 * dot(features, centers_t)
    return jnp.exp(-jnp.sqrt(jnp.maximum(distance, 0.0)) / kernel_length)


def step_kernel(
    n, nb, rank_rows, slot_rows,
    centers_h, weights_h, idx_h, basis_h, damping_h, pool_h, labels_h, picks_h,
    out_w, out_r,
    centers, weights, basis, pool, labels, idx_ref, damping_ref, picks_ref, idx_row, centers_t,
    feat, feat_f32, feat_all, pack_out, pack_in, place_out, place_in,
    sums_out, sums_in, back, back_f32, back_all,
    local_sem, send_sem, recv_sem,
):
    me, mb = lax.axis_index("center"), lax.axis_index("batch")
    own, D = feat.shape[1:]
    PC, C = weights.shape
    S, Q = basis_h.shape
    SP = basis.shape[0]
    pool_rows = pool.shape[0]
    group = own * n

    loads = [
        pltpu.make_async_copy(src, dst, local_sem.at[i])
        for i, (src, dst) in enumerate(
            [
                (picks_h, picks_ref),
                (pool_h, pool),
                (idx_h, idx_ref),
                (basis_h, basis.at[pl.ds(0, S)]),
                (centers_h, centers),
                (weights_h, weights),
                (labels_h, labels),
                (damping_h, damping_ref),
            ]
        )
    ]
    for load in loads:
        load.start()
    (picks_load, pool_load, idx_load, basis_load, centers_load, weights_load, labels_load, damping_load) = loads

    def center_peer(k):
        return lax.rem(me + 1 + k, n)

    def batch_peer(k):
        return lax.rem(mb + 1 + k, nb)

    barrier = pltpu.get_barrier_semaphore()

    def greet_center(k):
        pl.semaphore_signal(barrier, inc=1, device_id={"center": center_peer(k)}, device_id_type=MESH)

    def greet_batch(k):
        pl.semaphore_signal(barrier, inc=1, device_id={"batch": batch_peer(k)}, device_id_type=MESH)

    each(n - 1, greet_center)
    each(nb - 1, greet_batch)

    idx_row[...] = jnp.full(idx_row.shape, -1, jnp.int32)
    if SP > S:
        basis[pl.ds(S, SP - S), :] = jnp.zeros((SP - S, Q), BF16)
    if slot_rows > rank_rows:
        pack_in[:, pl.ds(rank_rows, slot_rows - rank_rows), :] = jnp.zeros(
            (n, slot_rows - rank_rows, Q), BF16
        )

    def send(src, dst, i, device):
        pltpu.make_async_remote_copy(
            src_ref=src,
            dst_ref=dst,
            send_sem=send_sem.at[i],
            recv_sem=recv_sem.at[i],
            device_id=device,
            device_id_type=MESH,
        ).start()

    def finish(sem, i, ref):
        pltpu.make_async_copy(ref, ref, sem.at[i]).wait()

    rest = pl.ds(0, n - 1)
    rest_b = pl.ds(0, nb - 1)
    head = pl.ds(0, rank_rows)

    picks_load.wait()
    pool_load.wait()
    picks = picks_ref[...]
    lanes = lax.broadcasted_iota(jnp.int32, (8, pool_rows), 1)
    rows = lax.broadcasted_iota(jnp.int32, (8, pool_rows), 0)
    pick = jnp.zeros((8, pool_rows), F32)
    for i in range(own):
        pick = pick + jnp.where((rows == i) & (lanes == picks[:, i : i + 1]), 1.0, 0.0)
    pick = pick.astype(BF16)
    feat[me] = dot(pick, pool[...])[0:own]

    pl.semaphore_wait(barrier, n + nb - 2)

    def send_feat(k):
        send(feat.at[me], feat.at[me], 0, {"center": center_peer(k)})

    each(n - 1, send_feat)

    idx_load.wait()
    idx_row[:, 0:S] = idx_ref[...]
    idx = idx_row[...]
    nh = round_up(n, 16)
    holders = lax.broadcasted_iota(jnp.int32, (nh, SP), 0)
    first = holders * PC
    inside = (idx >= first) & (idx < first + PC) & (holders < n)
    member = jnp.where(inside, 1.0, 0.0)
    before = jnp.where(
        lax.broadcasted_iota(jnp.int32, (SP, SP), 0) < lax.broadcasted_iota(jnp.int32, (SP, SP), 1), 1.0, 0.0
    )
    ranks = dot(member.astype(BF16), before.astype(BF16))
    rank = jnp.sum(member * ranks, axis=0, keepdims=True)
    packed_row = jnp.sum(member * (ranks + holders.astype(F32) * rank_rows + 1.0), axis=0, keepdims=True)
    share = LANES // slot_rows
    lane = rank + (lax.rem(me, share) * slot_rows).astype(F32)
    at_lane = lax.broadcasted_iota(jnp.int32, (LANES, SP), 0).astype(F32) == lane
    at_lane = jnp.where(at_lane, 1.0, 0.0).astype(BF16)
    local = idx - first + 1
    parts = [jnp.where(inside, p.astype(F32), 0.0) for p in (local >> 8, local & 255)]
    places = dot(jnp.concatenate(parts, axis=0).astype(BF16), at_lane, 1, 1)
    places = 256.0 * places[0:nh] + places[nh:]
    for h in range(n):
        place_out[h] = places[h : h + 1]
    place_in[me] = place_out[me]

    def send_place(k):
        j = center_peer(k)
        send(place_out.at[j], place_in.at[me], 2, {"center": j})

    each(n - 1, send_place)

    chosen = (lax.broadcasted_iota(jnp.int32, (n * rank_rows, SP), 0) + 1).astype(F32) == packed_row
    chosen = jnp.where(chosen, 1.0, 0.0).astype(BF16)
    basis_load.wait()
    pack_out[...] = dot(chosen, basis[...]).astype(BF16).reshape(n, rank_rows, Q)

    def send_pack(k):
        j = center_peer(k)
        send(pack_out.at[j], pack_in.at[me, head], 1, {"center": j})

    each(n - 1, send_pack)
    pack_in[me, pl.ds(0, rank_rows), :] = pack_out[me]

    centers_load.wait()
    centers_t[...] = jnp.transpose(centers[...])
    wide = centers_t[...].astype(F32)
    sq_centers = jnp.sum(wide * wide, axis=0, keepdims=True)

    finish(recv_sem, 0, feat.at[rest])
    for j in range(n):
        feat_f32[own * j : own * (j + 1), :] = feat[j]
    group_features = feat_f32[...].astype(BF16)
    feat_all[mb] = group_features
    kernel = laplace(group_features, sq_centers, centers_t[...]).astype(BF16)
    weights_load.wait()
    predicted = dot(kernel, weights[...])

    finish(recv_sem, 2, place_in.at[rest])
    tiles = []
    for t in range(round_up(n, share) // share):
        row = place_in[t * share]
        for j in range(t * share + 1, min(n, (t + 1) * share)):
            row = row + place_in[j]
        local_row = (lax.broadcasted_iota(jnp.int32, (PC, LANES), 0) + 1).astype(F32)
        tile = jnp.where(local_row == row, 1.0, 0.0).astype(BF16)
        tiles.append(tile[:, : min(n - t * share, share) * slot_rows])
    spread = jnp.concatenate(tiles, axis=1) if len(tiles) > 1 else tiles[0]
    picked = dot(kernel, spread).astype(BF16)
    finish(recv_sem, 1, pack_in.at[rest, head])
    packed = pack_in[...].reshape(n * slot_rows, Q)
    overlap = dot(picked, packed)

    for j in range(n):
        sums_out[j, :, 0:C] = predicted[own * j : own * (j + 1)]
        sums_out[j, :, C : C + Q] = overlap[own * j : own * (j + 1)]
    sums_in[me] = sums_out[me]

    def send_sums(k):
        j = center_peer(k)
        send(sums_out.at[j], sums_in.at[me], 3, {"center": j})

    def send_group(k):
        send(feat_all.at[mb], feat_all.at[mb], 4, {"batch": batch_peer(k)})

    each(n - 1, send_sums)
    each(nb - 1, send_group)
    own_basis = dot(spread, packed).astype(BF16)
    labels_load.wait()
    targets = dot(pick, labels[...])[0:own]
    damping_load.wait()
    scale = damping_ref[...] * step_rate

    finish(recv_sem, 3, sums_in.at[rest])
    total = jnp.sum(sums_in[...], axis=0)
    residual = (total[:, 0:C] - targets).astype(BF16)
    out_r[...] = residual
    back[me, :, 0:C] = residual.astype(F32)
    back[me, :, C : C + Q] = total[:, C:] * scale

    def send_back(k):
        send(back.at[me], back.at[me], 5, {"center": center_peer(k)})

    each(n - 1, send_back)

    finish(recv_sem, 4, feat_all.at[rest_b])
    all_features = feat_all[...].reshape(nb * group, D)
    twice = jnp.concatenate([all_features, all_features], axis=0)
    kernel_all = laplace(twice, sq_centers, centers_t[...]).astype(BF16).astype(F32)
    gradient_t = jnp.transpose(step_rate * kernel_all)

    finish(recv_sem, 5, back.at[rest])
    for j in range(n):
        back_f32[own * j : own * (j + 1), :] = back[j]
    overlap_f32 = back_f32[:, C : C + Q]
    overlap_high = overlap_f32.astype(BF16)
    back_all[mb, :, 0:C] = back_f32[:, 0:C].astype(BF16)
    back_all[mb, :, C : C + Q] = overlap_high
    back_all[mb, :, C + Q : C + 2 * Q] = (overlap_f32 - overlap_high.astype(F32)).astype(BF16)

    def send_back_batch(k):
        send(back_all.at[mb], back_all.at[mb], 6, {"batch": batch_peer(k)})

    each(nb - 1, send_back_batch)
    finish(recv_sem, 6, back_all.at[rest_b])

    everything = back_all[...].reshape(nb * group, C + 2 * Q)
    residuals = everything[:, 0:C]
    high, low = everything[:, C : C + Q], everything[:, C + Q :]
    mix = dot(own_basis, jnp.concatenate([high, high], axis=0), 1, 1)
    mix = mix + dot(own_basis, jnp.concatenate([low, low], axis=0), 1, 1) - gradient_t
    mix_high = mix.astype(BF16).astype(F32)
    is_high = lax.broadcasted_iota(jnp.int32, mix.shape, 1) < nb * group
    mix = jnp.where(is_high, mix_high, mix - mix_high).astype(BF16)
    change = dot(mix, jnp.concatenate([residuals, residuals], axis=0))
    out_w[...] = (weights[...].astype(F32) + change).astype(BF16)

    finish(send_sem, 0, feat.at[rest])
    finish(send_sem, 1, pack_in.at[rest, head])
    finish(send_sem, 2, place_in.at[rest])
    finish(send_sem, 3, sums_in.at[rest])
    finish(send_sem, 4, feat_all.at[rest_b])
    finish(send_sem, 5, back.at[rest])
    finish(send_sem, 6, back_all.at[rest_b])


def solution(mesh):
    n, nb = mesh.shape["center"], mesh.shape["batch"]

    def per_device(centers, weights, subset_index, basis, damping, stored, labels, picks):
        (PC, D), C = centers.shape, weights.shape[1]
        S, Q = basis.shape
        SP = round_up(S, LANES)
        own, pool_rows = picks.shape[1], stored.shape[1]
        group = own * n
        capacity = max(1, 4 * S // n)
        rank_rows = round_up(capacity, 16)
        slot_rows = 16
        while slot_rows < rank_rows:
            slot_rows *= 2
        hbm = pl.BlockSpec(memory_space=pltpu.HBM)
        vmem = pl.BlockSpec(memory_space=pltpu.VMEM)
        new_weights, residual = pl.pallas_call(
            functools.partial(step_kernel, n, nb, rank_rows, slot_rows),
            out_shape=(
                jax.ShapeDtypeStruct((PC, C), BF16),
                jax.ShapeDtypeStruct((own, C), BF16),
            ),
            in_specs=[hbm] * 8,
            out_specs=(vmem, vmem),
            scratch_shapes=[
                pltpu.VMEM((PC, D), BF16),
                pltpu.VMEM((PC, C), BF16),
                pltpu.VMEM((SP, Q), BF16),
                pltpu.VMEM((pool_rows, D), BF16),
                pltpu.VMEM((pool_rows, C), BF16),
                pltpu.VMEM((1, S), jnp.int32),
                pltpu.VMEM((1, Q), F32),
                pltpu.VMEM((1, own), jnp.int32),
                pltpu.VMEM((1, SP), jnp.int32),
                pltpu.VMEM((D, PC), BF16),
                pltpu.VMEM((n, own, D), F32),
                pltpu.VMEM((group, D), F32),
                pltpu.VMEM((nb, group, D), BF16),
                pltpu.VMEM((n, rank_rows, Q), BF16),
                pltpu.VMEM((n, slot_rows, Q), BF16),
                pltpu.VMEM((n, 1, LANES), F32),
                pltpu.VMEM((n, 1, LANES), F32),
                pltpu.VMEM((n, own, C + Q), F32),
                pltpu.VMEM((n, own, C + Q), F32),
                pltpu.VMEM((n, own, C + Q), F32),
                pltpu.VMEM((group, C + Q), F32),
                pltpu.VMEM((nb, group, C + 2 * Q), BF16),
                pltpu.SemaphoreType.DMA((8,)),
                pltpu.SemaphoreType.DMA((7,)),
                pltpu.SemaphoreType.DMA((7,)),
            ],
            compiler_params=pltpu.CompilerParams(
                collective_id=0, has_side_effects=True, vmem_limit_bytes=60 * 1024 * 1024
            ),
        )(
            centers,
            weights,
            subset_index.reshape(1, S),
            basis,
            damping.reshape(1, Q),
            stored[0],
            labels[0],
            picks,
        )
        return new_weights, residual[None]

    return jax.shard_map(
        per_device,
        mesh=mesh,
        in_specs=(
            P("center", None),
            P("center", None),
            P("center"),
            P("center", None),
            P(),
            P("batch", "center", None),
            P("batch", "center", None),
            P("batch", "center"),
        ),
        out_specs=(P("center", None), P("batch", "center", None)),
        check_vma=False,
    )
```

```python
import functools

import jax
import jax.numpy as jnp
from jax import lax
from jax.experimental import pallas as pl
from jax.experimental.pallas import tpu as pltpu
from jax.sharding import PartitionSpec as P

MESH = pl.DeviceIdType.MESH
kernel_length = 2.0
step_rate = 0.1
LANES = 128
F32, BF16 = jnp.float32, jnp.bfloat16


def dot(a, b, ca=1, cb=0):
    return lax.dot_general(a, b, (((ca,), (cb,)), ((), ())), preferred_element_type=F32)


def each(count, body):
    if count <= 8:
        for k in range(count):
            body(k)
    else:
        lax.fori_loop(0, count, lambda k, c: (body(k), c)[1], 0)


def round_up(x, m):
    return (x + m - 1) // m * m


def laplace(features, sq_centers, centers_t):
    wide = features.astype(F32)
    sq_samples = jnp.sum(wide * wide, axis=1, keepdims=True)
    distance = sq_samples + sq_centers - 2.0 * dot(features, centers_t)
    return jnp.exp(-jnp.sqrt(jnp.maximum(distance, 0.0)) / kernel_length)


def step_kernel(
    n, nb, rank_rows, slot_rows,
    centers_h, weights_h, idx_h, basis_h, damping_h, pool_h, labels_h, picks_h,
    out_w, out_r,
    centers, weights, basis, pool, labels, idx_ref, damping_ref, picks_ref, idx_row, centers_t,
    feat, feat_f32, feat_all, pack_out, pack_in, place_out, place_in,
    sums_out, sums_in, back, back_f32, back_all,
    local_sem, send_sem, recv_sem,
):
    me, mb = lax.axis_index("center"), lax.axis_index("batch")
    own, D = feat.shape[1:]
    PC, C = weights.shape
    S, Q = basis_h.shape
    SP = basis.shape[0]
    pool_rows = pool.shape[0]
    group = own * n

    loads = [
        pltpu.make_async_copy(src, dst, local_sem.at[i])
        for i, (src, dst) in enumerate(
            [
                (picks_h, picks_ref),
                (pool_h, pool),
                (idx_h, idx_ref),
                (basis_h, basis.at[pl.ds(0, S)]),
                (centers_h, centers),
                (weights_h, weights),
                (labels_h, labels),
                (damping_h, damping_ref),
            ]
        )
    ]
    for load in loads:
        load.start()
    (picks_load, pool_load, idx_load, basis_load, centers_load, weights_load, labels_load, damping_load) = loads

    def center_peer(k):
        return lax.rem(me + 1 + k, n)

    def batch_peer(k):
        return lax.rem(mb + 1 + k, nb)

    barrier = pltpu.get_barrier_semaphore()

    def greet_center(k):
        pl.semaphore_signal(barrier, inc=1, device_id={"center": center_peer(k)}, device_id_type=MESH)

    def greet_batch(k):
        pl.semaphore_signal(barrier, inc=1, device_id={"batch": batch_peer(k)}, device_id_type=MESH)

    each(n - 1, greet_center)
    each(nb - 1, greet_batch)

    idx_row[...] = jnp.full(idx_row.shape, -1, jnp.int32)
    if SP > S:
        basis[pl.ds(S, SP - S), :] = jnp.zeros((SP - S, Q), BF16)
    if slot_rows > rank_rows:
        pack_in[:, pl.ds(rank_rows, slot_rows - rank_rows), :] = jnp.zeros(
            (n, slot_rows - rank_rows, Q), BF16
        )

    def send(src, dst, i, device):
        pltpu.make_async_remote_copy(
            src_ref=src,
            dst_ref=dst,
            send_sem=send_sem.at[i],
            recv_sem=recv_sem.at[i],
            device_id=device,
            device_id_type=MESH,
        ).start()

    def finish(sem, i, ref):
        pltpu.make_async_copy(ref, ref, sem.at[i]).wait()

    rest = pl.ds(0, n - 1)
    rest_b = pl.ds(0, nb - 1)
    head = pl.ds(0, rank_rows)

    picks_load.wait()
    pool_load.wait()
    picks = picks_ref[...]
    lanes = lax.broadcasted_iota(jnp.int32, (8, pool_rows), 1)
    rows = lax.broadcasted_iota(jnp.int32, (8, pool_rows), 0)
    pick = jnp.zeros((8, pool_rows), F32)
    for i in range(own):
        pick = pick + jnp.where((rows == i) & (lanes == picks[:, i : i + 1]), 1.0, 0.0)
    pick = pick.astype(BF16)
    feat[me] = dot(pick, pool[...])[0:own]

    pl.semaphore_wait(barrier, n + nb - 2)

    def send_feat(k):
        send(feat.at[me], feat.at[me], 0, {"center": center_peer(k)})

    each(n - 1, send_feat)

    idx_load.wait()
    idx_row[:, 0:S] = idx_ref[...]
    idx = idx_row[...]
    nh = round_up(n, 16)
    holders = lax.broadcasted_iota(jnp.int32, (nh, SP), 0)
    first = holders * PC
    inside = (idx >= first) & (idx < first + PC) & (holders < n)
    member = jnp.where(inside, 1.0, 0.0)
    before = jnp.where(
        lax.broadcasted_iota(jnp.int32, (SP, SP), 0) < lax.broadcasted_iota(jnp.int32, (SP, SP), 1), 1.0, 0.0
    )
    ranks = dot(member.astype(BF16), before.astype(BF16))
    rank = jnp.sum(member * ranks, axis=0, keepdims=True)
    packed_row = jnp.sum(member * (ranks + holders.astype(F32) * rank_rows + 1.0), axis=0, keepdims=True)
    share = LANES // slot_rows
    lane = rank + (lax.rem(me, share) * slot_rows).astype(F32)
    at_lane = lax.broadcasted_iota(jnp.int32, (LANES, SP), 0).astype(F32) == lane
    at_lane = jnp.where(at_lane, 1.0, 0.0).astype(BF16)
    local = idx - first + 1
    parts = [jnp.where(inside, p.astype(F32), 0.0) for p in (local >> 8, local & 255)]
    places = dot(jnp.concatenate(parts, axis=0).astype(BF16), at_lane, 1, 1)
    places = 256.0 * places[0:nh] + places[nh:]
    for h in range(n):
        place_out[h] = places[h : h + 1]
    place_in[me] = place_out[me]

    def send_place(k):
        j = center_peer(k)
        send(place_out.at[j], place_in.at[me], 2, {"center": j})

    each(n - 1, send_place)

    chosen = (lax.broadcasted_iota(jnp.int32, (n * rank_rows, SP), 0) + 1).astype(F32) == packed_row
    chosen = jnp.where(chosen, 1.0, 0.0).astype(BF16)
    basis_load.wait()
    pack_out[...] = dot(chosen, basis[...]).astype(BF16).reshape(n, rank_rows, Q)

    def send_pack(k):
        j = center_peer(k)
        send(pack_out.at[j], pack_in.at[me, head], 1, {"center": j})

    each(n - 1, send_pack)
    pack_in[me, pl.ds(0, rank_rows), :] = pack_out[me]

    centers_load.wait()
    centers_t[...] = jnp.transpose(centers[...])
    wide = centers_t[...].astype(F32)
    sq_centers = jnp.sum(wide * wide, axis=0, keepdims=True)

    finish(recv_sem, 0, feat.at[rest])
    for j in range(n):
        feat_f32[own * j : own * (j + 1), :] = feat[j]
    group_features = feat_f32[...].astype(BF16)
    feat_all[mb] = group_features
    kernel = laplace(group_features, sq_centers, centers_t[...]).astype(BF16)
    weights_load.wait()
    predicted = dot(kernel, weights[...])

    finish(recv_sem, 2, place_in.at[rest])
    tiles = []
    for t in range(round_up(n, share) // share):
        row = place_in[t * share]
        for j in range(t * share + 1, min(n, (t + 1) * share)):
            row = row + place_in[j]
        local_row = (lax.broadcasted_iota(jnp.int32, (PC, LANES), 0) + 1).astype(F32)
        tile = jnp.where(local_row == row, 1.0, 0.0).astype(BF16)
        tiles.append(tile[:, : min(n - t * share, share) * slot_rows])
    spread = jnp.concatenate(tiles, axis=1) if len(tiles) > 1 else tiles[0]
    picked = dot(kernel, spread).astype(BF16)
    finish(recv_sem, 1, pack_in.at[rest, head])
    packed = pack_in[...].reshape(n * slot_rows, Q)
    overlap = dot(picked, packed)

    for j in range(n):
        sums_out[j, :, 0:C] = predicted[own * j : own * (j + 1)]
        sums_out[j, :, C : C + Q] = overlap[own * j : own * (j + 1)]
    sums_in[me] = sums_out[me]

    def send_sums(k):
        j = center_peer(k)
        send(sums_out.at[j], sums_in.at[me], 3, {"center": j})

    def send_group(k):
        send(feat_all.at[mb], feat_all.at[mb], 4, {"batch": batch_peer(k)})

    each(n - 1, send_sums)
    each(nb - 1, send_group)
    own_basis = dot(spread, packed).astype(BF16)
    labels_load.wait()
    targets = dot(pick, labels[...])[0:own]
    damping_load.wait()
    scale = damping_ref[...] * step_rate

    finish(recv_sem, 3, sums_in.at[rest])
    total = jnp.sum(sums_in[...], axis=0)
    residual = (total[:, 0:C] - targets).astype(BF16)
    out_r[...] = residual
    back[me, :, 0:C] = residual.astype(F32)
    back[me, :, C : C + Q] = total[:, C:] * scale

    def send_back(k):
        send(back.at[me], back.at[me], 5, {"center": center_peer(k)})

    each(n - 1, send_back)

    finish(recv_sem, 4, feat_all.at[rest_b])
    all_features = feat_all[...].reshape(nb * group, D)
    twice = jnp.concatenate([all_features, all_features], axis=0)
    kernel_all = laplace(twice, sq_centers, centers_t[...]).astype(BF16).astype(F32)
    gradient_t = jnp.transpose(step_rate * kernel_all)

    finish(recv_sem, 5, back.at[rest])
    for j in range(n):
        back_f32[own * j : own * (j + 1), :] = back[j]
    overlap_f32 = back_f32[:, C : C + Q]
    overlap_high = overlap_f32.astype(BF16)
    back_all[mb, :, 0:C] = back_f32[:, 0:C].astype(BF16)
    back_all[mb, :, C : C + Q] = overlap_high
    back_all[mb, :, C + Q : C + 2 * Q] = (overlap_f32 - overlap_high.astype(F32)).astype(BF16)

    def send_back_batch(k):
        send(back_all.at[mb], back_all.at[mb], 6, {"batch": batch_peer(k)})

    each(nb - 1, send_back_batch)
    finish(recv_sem, 6, back_all.at[rest_b])

    everything = back_all[...].reshape(nb * group, C + 2 * Q)
    residuals = everything[:, 0:C]
    high, low = everything[:, C : C + Q], everything[:, C + Q :]
    mix = dot(own_basis, jnp.concatenate([high, high], axis=0), 1, 1)
    mix = mix + dot(own_basis, jnp.concatenate([low, low], axis=0), 1, 1) - gradient_t
    mix_high = mix.astype(BF16).astype(F32)
    is_high = lax.broadcasted_iota(jnp.int32, mix.shape, 1) < nb * group
    mix = jnp.where(is_high, mix_high, mix - mix_high).astype(BF16)
    change = dot(mix, jnp.concatenate([residuals, residuals], axis=0))
    out_w[...] = (weights[...].astype(F32) + change).astype(BF16)

    finish(send_sem, 0, feat.at[rest])
    finish(send_sem, 1, pack_in.at[rest, head])
    finish(send_sem, 2, place_in.at[rest])
    finish(send_sem, 3, sums_in.at[rest])
    finish(send_sem, 4, feat_all.at[rest_b])
    finish(send_sem, 5, back.at[rest])
    finish(send_sem, 6, back_all.at[rest_b])


def solution(mesh):
    n, nb = mesh.shape["center"], mesh.shape["batch"]

    def per_device(centers, weights, subset_index, basis, damping, stored, labels, picks):
        (PC, D), C = centers.shape, weights.shape[1]
        S, Q = basis.shape
        SP = round_up(S, LANES)
        own, pool_rows = picks.shape[1], stored.shape[1]
        group = own * n
        capacity = max(1, 4 * S // n)
        rank_rows = round_up(capacity, 16)
        slot_rows = 16
        while slot_rows < rank_rows:
            slot_rows *= 2
        hbm = pl.BlockSpec(memory_space=pltpu.HBM)
        vmem = pl.BlockSpec(memory_space=pltpu.VMEM)
        new_weights, residual = pl.pallas_call(
            functools.partial(step_kernel, n, nb, rank_rows, slot_rows),
            out_shape=(
                pltpu.VMEM((PC, C), BF16),
                pltpu.VMEM((own, C), BF16),
            ),
            in_specs=[hbm] * 8,
            out_specs=(vmem, vmem),
            scratch_shapes=[
                pltpu.VMEM((PC, D), BF16),
                pltpu.VMEM((PC, C), BF16),
                pltpu.VMEM((SP, Q), BF16),
                pltpu.VMEM((pool_rows, D), BF16),
                pltpu.VMEM((pool_rows, C), BF16),
                pltpu.VMEM((1, S), jnp.int32),
                pltpu.VMEM((1, Q), F32),
                pltpu.VMEM((1, own), jnp.int32),
                pltpu.VMEM((1, SP), jnp.int32),
                pltpu.VMEM((D, PC), BF16),
                pltpu.VMEM((n, own, D), F32),
                pltpu.VMEM((group, D), F32),
                pltpu.VMEM((nb, group, D), BF16),
                pltpu.VMEM((n, rank_rows, Q), BF16),
                pltpu.VMEM((n, slot_rows, Q), BF16),
                pltpu.VMEM((n, 1, LANES), F32),
                pltpu.VMEM((n, 1, LANES), F32),
                pltpu.VMEM((n, own, C + Q), F32),
                pltpu.VMEM((n, own, C + Q), F32),
                pltpu.VMEM((n, own, C + Q), F32),
                pltpu.VMEM((group, C + Q), F32),
                pltpu.VMEM((nb, group, C + 2 * Q), BF16),
                pltpu.SemaphoreType.DMA((8,)),
                pltpu.SemaphoreType.DMA((7,)),
                pltpu.SemaphoreType.DMA((7,)),
            ],
            compiler_params=pltpu.CompilerParams(
                collective_id=0, has_side_effects=True, vmem_limit_bytes=60 * 1024 * 1024
            ),
        )(
            centers,
            weights,
            subset_index.reshape(1, S),
            basis,
            damping.reshape(1, Q),
            stored[0],
            labels[0],
            picks,
        )
        return new_weights, residual[None]

    return jax.shard_map(
        per_device,
        mesh=mesh,
        in_specs=(
            P("center", None),
            P("center", None),
            P("center"),
            P("center", None),
            P(),
            P("batch", "center", None),
            P("batch", "center", None),
            P("batch", "center"),
        ),
        out_specs=(P("center", None), P("batch", "center", None)),
        check_vma=False,
    )
```

```python
import functools

import jax
import jax.numpy as jnp
from jax import lax
from jax.experimental import pallas as pl
from jax.experimental.pallas import tpu as pltpu
from jax.sharding import PartitionSpec as P

MESH = pl.DeviceIdType.MESH
kernel_length = 2.0
step_rate = 0.1
LANES = 128
F32, BF16 = jnp.float32, jnp.bfloat16


def dot(a, b, ca=1, cb=0):
    return lax.dot_general(a, b, (((ca,), (cb,)), ((), ())), preferred_element_type=F32)


def each(count, body):
    if count <= 8:
        for k in range(count):
            body(k)
    else:
        lax.fori_loop(0, count, lambda k, c: (body(k), c)[1], 0)


def round_up(x, m):
    return (x + m - 1) // m * m


def laplace(features, sq_centers, centers_t):
    wide = features.astype(F32)
    sq_samples = jnp.sum(wide * wide, axis=1, keepdims=True)
    distance = sq_samples + sq_centers - 2.0 * dot(features, centers_t)
    return jnp.exp(-jnp.sqrt(jnp.maximum(distance, 0.0)) / kernel_length)


def step_kernel(
    n, nb, rank_rows, slot_rows,
    centers_h, weights_h, idx_h, basis_h, damping_h, pool_h, labels_h, picks_h,
    out_w, out_r,
    centers, weights, basis, pool, labels, idx_ref, damping_ref, picks_ref, idx_row, centers_t,
    feat, feat_f32, feat_all, pack_out, pack_in, place_out, place_in,
    sums_out, sums_in, back, back_f32, back_all,
    local_sem, send_sem, recv_sem,
):
    me, mb = lax.axis_index("center"), lax.axis_index("batch")
    own, D = feat.shape[1:]
    PC, C = weights.shape
    S, Q = basis_h.shape
    Qh = Q // 2
    half = lax.rem(mb, 2)
    pair = mb + 1 - 2 * half
    columns = pl.ds(pl.multiple_of(half * Qh, Qh), Qh)
    SP = basis.shape[0]
    pool_rows = pool.shape[0]
    group = own * n

    loads = [
        pltpu.make_async_copy(src, dst, local_sem.at[i])
        for i, (src, dst) in enumerate(
            [
                (picks_h, picks_ref),
                (pool_h, pool),
                (idx_h, idx_ref),
                (basis_h.at[:, columns], basis.at[pl.ds(0, S)]),
                (centers_h, centers),
                (weights_h, weights),
                (labels_h, labels),
                (damping_h.at[:, columns], damping_ref),
            ]
        )
    ]
    for load in loads:
        load.start()
    (picks_load, pool_load, idx_load, basis_load, centers_load, weights_load, labels_load, damping_load) = loads

    def center_peer(k):
        return lax.rem(me + 1 + k, n)

    def batch_peer(k):
        return lax.rem(mb + 1 + k, nb)

    barrier = pltpu.get_barrier_semaphore()

    def greet_center(k):
        pl.semaphore_signal(barrier, inc=1, device_id={"center": center_peer(k)}, device_id_type=MESH)

    def greet_batch(k):
        pl.semaphore_signal(barrier, inc=1, device_id={"batch": batch_peer(k)}, device_id_type=MESH)

    each(n - 1, greet_center)
    each(nb - 1, greet_batch)

    idx_row[...] = jnp.full(idx_row.shape, -1, jnp.int32)
    if SP > S:
        basis[pl.ds(S, SP - S), :] = jnp.zeros((SP - S, Qh), BF16)
    if slot_rows > rank_rows:
        pack_in[half, :, pl.ds(rank_rows, slot_rows - rank_rows), :] = jnp.zeros(
            (n, slot_rows - rank_rows, Qh), BF16
        )

    def send(src, dst, i, device):
        pltpu.make_async_remote_copy(
            src_ref=src,
            dst_ref=dst,
            send_sem=send_sem.at[i],
            recv_sem=recv_sem.at[i],
            device_id=device,
            device_id_type=MESH,
        ).start()

    def finish(sem, i, ref):
        pltpu.make_async_copy(ref, ref, sem.at[i]).wait()

    rest = pl.ds(0, n - 1)
    rest_b = pl.ds(0, nb - 1)
    head = pl.ds(0, rank_rows)

    picks_load.wait()
    pool_load.wait()
    picks = picks_ref[...]
    lanes = lax.broadcasted_iota(jnp.int32, (8, pool_rows), 1)
    rows = lax.broadcasted_iota(jnp.int32, (8, pool_rows), 0)
    pick = jnp.zeros((8, pool_rows), F32)
    for i in range(own):
        pick = pick + jnp.where((rows == i) & (lanes == picks[:, i : i + 1]), 1.0, 0.0)
    pick = pick.astype(BF16)
    feat[me] = dot(pick, pool[...])[0:own]

    pl.semaphore_wait(barrier, n + nb - 2)

    def send_feat(k):
        send(feat.at[me], feat.at[me], 0, {"center": center_peer(k)})

    each(n - 1, send_feat)

    idx_load.wait()
    idx_row[:, 0:S] = idx_ref[...]
    idx = idx_row[...]
    nh = round_up(n, 16)
    holders = lax.broadcasted_iota(jnp.int32, (nh, SP), 0)
    first = holders * PC
    inside = (idx >= first) & (idx < first + PC) & (holders < n)
    member = jnp.where(inside, 1.0, 0.0)
    before = jnp.where(
        lax.broadcasted_iota(jnp.int32, (SP, SP), 0) < lax.broadcasted_iota(jnp.int32, (SP, SP), 1), 1.0, 0.0
    )
    ranks = dot(member.astype(BF16), before.astype(BF16))
    rank = jnp.sum(member * ranks, axis=0, keepdims=True)
    packed_row = jnp.sum(member * (ranks + holders.astype(F32) * rank_rows + 1.0), axis=0, keepdims=True)
    share = LANES // slot_rows
    lane = rank + (lax.rem(me, share) * slot_rows).astype(F32)
    at_lane = lax.broadcasted_iota(jnp.int32, (LANES, SP), 0).astype(F32) == lane
    at_lane = jnp.where(at_lane, 1.0, 0.0).astype(BF16)
    local = idx - first + 1
    parts = [jnp.where(inside, p.astype(F32), 0.0) for p in (local >> 8, local & 255)]
    places = dot(jnp.concatenate(parts, axis=0).astype(BF16), at_lane, 1, 1)
    places = 256.0 * places[0:nh] + places[nh:]
    for h in range(n):
        place_out[h] = places[h : h + 1]
    place_in[me] = place_out[me]

    def send_place(k):
        j = center_peer(k)
        send(place_out.at[j], place_in.at[me], 2, {"center": j})

    each(n - 1, send_place)

    chosen = (lax.broadcasted_iota(jnp.int32, (n * rank_rows, SP), 0) + 1).astype(F32) == packed_row
    chosen = jnp.where(chosen, 1.0, 0.0).astype(BF16)
    basis_load.wait()
    pack_out[...] = dot(chosen, basis[...]).astype(BF16).reshape(n, rank_rows, Qh)

    def send_pack(k):
        j = center_peer(k)
        send(pack_out.at[j], pack_in.at[half, me, head], 1, {"center": j})

    each(n - 1, send_pack)
    pack_in[half, me, pl.ds(0, rank_rows), :] = pack_out[me]

    centers_load.wait()
    centers_t[...] = jnp.transpose(centers[...])
    wide = centers_t[...].astype(F32)
    sq_centers = jnp.sum(wide * wide, axis=0, keepdims=True)

    finish(recv_sem, 0, feat.at[rest])
    for j in range(n):
        feat_f32[own * j : own * (j + 1), :] = feat[j]
    group_features = feat_f32[...].astype(BF16)
    feat_all[mb] = group_features
    send(feat_all.at[mb], feat_all.at[mb], 7, {"batch": pair})
    kernel = laplace(group_features, sq_centers, centers_t[...]).astype(BF16)
    weights_load.wait()
    predicted = dot(kernel, weights[...])

    def send_group(k):
        other = lax.rem(mb - half + 2 + k, nb)
        send(feat_all.at[mb], feat_all.at[mb], 4, {"batch": other})

    each(nb - 2, send_group)

    finish(recv_sem, 2, place_in.at[rest])
    tiles = []
    for t in range(round_up(n, share) // share):
        row = place_in[t * share]
        for j in range(t * share + 1, min(n, (t + 1) * share)):
            row = row + place_in[j]
        local_row = (lax.broadcasted_iota(jnp.int32, (PC, LANES), 0) + 1).astype(F32)
        tile = jnp.where(local_row == row, 1.0, 0.0).astype(BF16)
        tiles.append(tile[:, : min(n - t * share, share) * slot_rows])
    spread = jnp.concatenate(tiles, axis=1) if len(tiles) > 1 else tiles[0]
    finish(recv_sem, 7, feat_all.at[0])
    pair_kernel = laplace(feat_all[pair], sq_centers, centers_t[...]).astype(BF16)
    picked = dot(jnp.concatenate([kernel, pair_kernel], axis=0), spread).astype(BF16)
    finish(recv_sem, 1, pack_in.at[0, rest, head])
    packed = pack_in[half].reshape(n * slot_rows, Qh)
    overlap = dot(picked, packed)

    for j in range(n):
        sums_out[j, :, 0:C] = predicted[own * j : own * (j + 1)]
        sums_out[j, :, C : C + Qh] = overlap[own * j : own * (j + 1)]
        sums_out[j, :, C + Qh :] = overlap[group + own * j : group + own * (j + 1)]
    sums_in[me] = sums_out[me]

    def send_sums(k):
        j = center_peer(k)
        send(sums_out.at[j], sums_in.at[me], 3, {"center": j})

    each(n - 1, send_sums)
    send(pack_in.at[half], pack_in.at[half], 8, {"batch": pair})
    labels_load.wait()
    targets = dot(pick, labels[...])[0:own]
    damping_load.wait()
    scale = damping_ref[...] * step_rate
    scale = jnp.concatenate([scale, scale], axis=1)

    finish(recv_sem, 3, sums_in.at[rest])
    total = jnp.sum(sums_in[...], axis=0)
    residual = (total[:, 0:C] - targets).astype(BF16)
    out_r[...] = residual
    back[me, :, 0:C] = residual.astype(F32)
    back[me, :, C : C + Q] = total[:, C:] * scale

    def send_back(k):
        send(back.at[me], back.at[me], 5, {"center": center_peer(k)})

    each(n - 1, send_back)

    finish(recv_sem, 8, pack_in.at[0])
    own_basis = jnp.concatenate(
        [dot(spread, pack_in[q].reshape(n * slot_rows, Qh)).astype(BF16) for q in range(2)], axis=1
    )
    finish(recv_sem, 4, feat_all.at[pl.ds(0, nb - 2)])
    all_features = feat_all[...].reshape(nb * group, D)
    twice = jnp.concatenate([all_features, all_features], axis=0)
    kernel_all = laplace(twice, sq_centers, centers_t[...]).astype(BF16).astype(F32)
    gradient_t = jnp.transpose(step_rate * kernel_all)

    finish(recv_sem, 5, back.at[rest])
    for j in range(n):
        back_f32[own * j : own * (j + 1), :] = back[j]
    overlap_f32 = back_f32[:, C : C + Q]
    overlap_high = overlap_f32.astype(BF16)
    back_all[mb, :, 0:C] = back_f32[:, 0:C].astype(BF16)
    back_all[mb, :, C : C + Q] = overlap_high
    back_all[mb, :, C + Q : C + 2 * Q] = (overlap_f32 - overlap_high.astype(F32)).astype(BF16)

    def send_back_batch(k):
        send(back_all.at[mb], back_all.at[mb], 6, {"batch": batch_peer(k)})

    each(nb - 1, send_back_batch)
    finish(recv_sem, 6, back_all.at[rest_b])

    residuals = back_all[:, :, 0:C].reshape(nb * group, C)

    def overlap_part(start):
        rows = []
        for g in range(nb):
            halves = []
            for q in range(2):
                at = start + (0 if q == g % 2 else Qh)
                halves.append(back_all[g - g % 2 + q, :, at : at + Qh])
            rows.append(jnp.concatenate(halves, axis=1))
        return jnp.concatenate(rows, axis=0)

    high, low = overlap_part(C), overlap_part(C + Q)
    mix = dot(own_basis, jnp.concatenate([high, high], axis=0), 1, 1)
    mix = mix + dot(own_basis, jnp.concatenate([low, low], axis=0), 1, 1) - gradient_t
    mix_high = mix.astype(BF16).astype(F32)
    is_high = lax.broadcasted_iota(jnp.int32, mix.shape, 1) < nb * group
    mix = jnp.where(is_high, mix_high, mix - mix_high).astype(BF16)
    change = dot(mix, jnp.concatenate([residuals, residuals], axis=0))
    out_w[...] = (weights[...].astype(F32) + change).astype(BF16)

    finish(send_sem, 0, feat.at[rest])
    finish(send_sem, 1, pack_in.at[0, rest, head])
    finish(send_sem, 2, place_in.at[rest])
    finish(send_sem, 3, sums_in.at[rest])
    finish(send_sem, 4, feat_all.at[pl.ds(0, nb - 2)])
    finish(send_sem, 7, feat_all.at[0])
    finish(send_sem, 8, pack_in.at[0])
    finish(send_sem, 5, back.at[rest])
    finish(send_sem, 6, back_all.at[rest_b])


def solution(mesh):
    n, nb = mesh.shape["center"], mesh.shape["batch"]

    def per_device(centers, weights, subset_index, basis, damping, stored, labels, picks):
        (PC, D), C = centers.shape, weights.shape[1]
        S, Q = basis.shape
        SP = round_up(S, LANES)
        own, pool_rows = picks.shape[1], stored.shape[1]
        group = own * n
        capacity = max(1, 4 * S // n)
        rank_rows = round_up(capacity, 16)
        slot_rows = 16
        while slot_rows < rank_rows:
            slot_rows *= 2
        hbm = pl.BlockSpec(memory_space=pltpu.HBM)
        vmem = pl.BlockSpec(memory_space=pltpu.VMEM)
        new_weights, residual = pl.pallas_call(
            functools.partial(step_kernel, n, nb, rank_rows, slot_rows),
            out_shape=(
                pltpu.VMEM((PC, C), BF16),
                pltpu.VMEM((own, C), BF16),
            ),
            in_specs=[hbm] * 8,
            out_specs=(vmem, vmem),
            scratch_shapes=[
                pltpu.VMEM((PC, D), BF16),
                pltpu.VMEM((PC, C), BF16),
                pltpu.VMEM((SP, Q // 2), BF16),
                pltpu.VMEM((pool_rows, D), BF16),
                pltpu.VMEM((pool_rows, C), BF16),
                pltpu.VMEM((1, S), jnp.int32),
                pltpu.VMEM((1, Q // 2), F32),
                pltpu.VMEM((1, own), jnp.int32),
                pltpu.VMEM((1, SP), jnp.int32),
                pltpu.VMEM((D, PC), BF16),
                pltpu.VMEM((n, own, D), F32),
                pltpu.VMEM((group, D), F32),
                pltpu.VMEM((nb, group, D), BF16),
                pltpu.VMEM((n, rank_rows, Q // 2), BF16),
                pltpu.VMEM((2, n, slot_rows, Q // 2), BF16),
                pltpu.VMEM((n, 1, LANES), F32),
                pltpu.VMEM((n, 1, LANES), F32),
                pltpu.VMEM((n, own, C + Q), F32),
                pltpu.VMEM((n, own, C + Q), F32),
                pltpu.VMEM((n, own, C + Q), F32),
                pltpu.VMEM((group, C + Q), F32),
                pltpu.VMEM((nb, group, C + 2 * Q), BF16),
                pltpu.SemaphoreType.DMA((8,)),
                pltpu.SemaphoreType.DMA((9,)),
                pltpu.SemaphoreType.DMA((9,)),
            ],
            compiler_params=pltpu.CompilerParams(
                collective_id=0, has_side_effects=True, vmem_limit_bytes=60 * 1024 * 1024
            ),
        )(
            centers,
            weights,
            subset_index.reshape(1, S),
            basis,
            damping.reshape(1, Q),
            stored[0],
            labels[0],
            picks,
        )
        return new_weights, residual[None]

    return jax.shard_map(
        per_device,
        mesh=mesh,
        in_specs=(
            P("center", None),
            P("center", None),
            P("center"),
            P("center", None),
            P(),
            P("batch", "center", None),
            P("batch", "center", None),
            P("batch", "center"),
        ),
        out_specs=(P("center", None), P("batch", "center", None)),
        check_vma=False,
    )
```
